128 devices in a mesh: row: 32 (over y, z, core), col: 4 (over x).
Axes of the slice: x: 4, y: 4, z: 4, core: 2. Of those that a mesh axis runs over, the one named last changes fastest.
Arguments:
- points: bfloat16 [64, 65536], P(None, ('row', 'col')), may hold values from -6 to 6
- lengths: float32 [64], replicated, may hold values from 0.5 to 2
- noise_var: float32 [65536], P(('row', 'col')), may hold values from 0.1 to 1
- solution: float32 [16, 65536], P(None, ('row', 'col')), may hold values from -6 to 6
- residual: float32 [16, 65536], P(None, ('row', 'col')), may hold values from -100 to 100
- direction: float32 [16, 65536], P(None, ('row', 'col')), may hold values from -100 to 100
Outputs:
- new_solution: float32 [16, 65536], P(None, ('row', 'col'))
- new_residual: float32 [16, 65536], P(None, ('row', 'col'))
- new_direction: float32 [16, 65536], P(None, ('row', 'col'))
The draws below stay inside these ranges and needn't reach their ends.
All inputs are finite; a program needn't handle non-finite values.
Results may differ from the reference program's by a relative error of at most 0.0043.
Values may be sent and summed in bfloat16 or wider, within the bound.
A program may use at most 64 MiB of HBM per device.

```python
import math
import jax
import jax.numpy as jnp
from jax import lax

FEAT = 64
RHS = 16
POINTS = 65536


def scaled_field(key, top_scale):
    key_base = jax.random.fold_in(key, 0)
    key_rows = jax.random.fold_in(key, 2)
    key_cols = jax.random.fold_in(key, 3)
    base_draw = jax.random.truncated_normal(key_base, -4.0, 4.0, (RHS, POINTS), jnp.float32)
    mixed_draw = base_draw
    position = jnp.arange(POINTS, dtype=jnp.float32) / POINTS
    row_scale = jnp.exp(jax.random.uniform(key_rows, (POINTS,), jnp.float32, 0.0, math.log(top_scale)) + math.log(3.0) * position)
    col_scale = jnp.exp(jax.random.uniform(key_cols, (RHS, 1), jnp.float32, 0.0, math.log(10.0)))
    return mixed_draw * row_scale[None, :] * col_scale * 0.05


def draw_points(key, part):
    key = jax.random.fold_in(key, 11)
    key_latent, key_coef, key_jitter = jax.random.split(key, 3)
    span_size = 2.5
    latent = jax.random.uniform(key_latent, (4, POINTS), jnp.float32, -0.5, 0.5) * span_size
    coefficient = 0.25 * jax.random.uniform(key_coef, (FEAT,), jnp.float32, 0.6, 1.4)
    jitter = 0.1 * jax.random.truncated_normal(key_jitter, -4.0, 4.0, (FEAT, POINTS), jnp.float32)
    values = jnp.tile(latent, (FEAT // 4, 1)) * coefficient[:, None] + jitter
    return values.astype(jnp.bfloat16)


def draw_residual(key, part):
    key = jax.random.fold_in(key, 17)
    return scaled_field(key, 10.0)


def draw_direction(key, part):
    key = jax.random.fold_in(key, 23)
    return scaled_field(key, 10.0)


def steps_of(key, extent, cuts, least, top_value):
    level, own = 1.0, jax.random.fold_in(key, 6)
    for axis_at, parts in cuts:
        heights = jnp.exp(jax.random.uniform(jax.random.fold_in(own, axis_at), (parts,), jnp.float32, least / len(cuts), top_value / len(cuts)))
        level = level * jnp.repeat(heights, extent[axis_at] // parts).reshape([-1 if axis == axis_at else 1 for axis in range(len(extent))])
    return level


def scatter_about(own_key, extent, deviation, reach, cuts=(), kind=jnp.bfloat16):
    array = deviation * jax.random.normal(own_key, extent, jnp.float32)
    if cuts:
        array = array * steps_of(own_key, extent, cuts, -0.22, 0.18)
    return jnp.clip(array, -reach, reach).astype(kind)


def setup_inputs(seed: int = 0) -> dict:
    seeds = jax.random.split(jax.random.key(seed), 7)
    points = draw_points(jax.random.fold_in(seeds[6], 71), 0)
    lengths = jnp.clip(jnp.exp(jax.random.uniform(seeds[1], (FEAT,), jnp.float32, math.log(0.5), math.log(2.0))), 0.5, 2.0)
    noise_var = jnp.clip(jnp.exp(math.log(1.0) - 2.3025851 * jax.random.uniform(seeds[2], (POINTS,), jnp.float32) ** steps_of(seeds[2], (POINTS,), ((0, 128),), -0.2, 0.2)), 0.1, 1.0)
    solution = scatter_about(seeds[3], (RHS, POINTS), 1.0, 6.0, ((1, 128),), jnp.float32)
    residual = draw_residual(jax.random.fold_in(seeds[6], 71), 0)
    direction = draw_direction(jax.random.fold_in(seeds[6], 71), 0)
    return {"points": points, "lengths": lengths, "noise_var": noise_var, "solution": solution, "residual": residual, "direction": direction}


def reference(points, lengths, noise_var, solution, residual, direction):
    scaled = (points.astype(jnp.float32) / lengths[:, None]).astype(jnp.bfloat16)
    values = scaled.astype(jnp.float32)
    squares = jnp.sum(values * values, axis=0)
    narrow = direction.astype(jnp.bfloat16)
    block_rows = math.gcd(POINTS, 1024)

    def block_image(begin):
        part_scaled = lax.dynamic_slice_in_dim(scaled, begin, block_rows, 1)
        part_sq = lax.dynamic_slice_in_dim(squares, begin, block_rows, 0)
        cross_term = lax.dot_general(part_scaled, scaled, (((0,), (0,)), ((), ())), preferred_element_type=jnp.float32)
        kernel_tile = jnp.exp(-0.5 * (part_sq[:, None] + squares[None, :] - 2.0 * cross_term)).astype(jnp.bfloat16)
        return lax.dot_general(narrow, kernel_tile, (((1,), (1,)), ((), ())), preferred_element_type=jnp.float32)

    starts = jnp.arange(POINTS // block_rows, dtype=jnp.int32) * block_rows
    pieces = lax.map(block_image, starts)
    kernel_part = jnp.transpose(pieces, (1, 0, 2)).reshape(RHS, POINTS)
    image_field = kernel_part + noise_var[None, :] * direction
    norm_old = jnp.sum(residual * residual, axis=1)
    curvature = jnp.sum(direction * image_field, axis=1)
    step_size = norm_old / curvature
    new_solution = solution + step_size[:, None] * direction
    new_residual = residual - step_size[:, None] * image_field
    norm_new = jnp.sum(new_residual * new_residual, axis=1)
    new_direction = new_residual + (norm_new / norm_old)[:, None] * direction
    return (new_solution, new_residual, new_direction)
```

```python
import functools

import jax
import jax.numpy as jnp
from jax import lax
from jax.experimental import pallas as pl
from jax.experimental.pallas import tpu as pltpu
from jax.sharding import PartitionSpec as P

MESH = pl.DeviceIdType.MESH
FEAT = 64
RHS = 16
DEEP = FEAT + 16
ROWS = DEEP + RHS
SIDE = 4


def plane_order():
    hops = lambda d: min(d, SIDE - d)
    pairs = [(a, b) for a in range(SIDE) for b in range(SIDE)]
    return sorted(pairs, key=lambda p: (hops(p[0]) + hops(p[1]), p))


def bias_rows(scaled, flip):
    values = scaled.astype(jnp.float32)
    half = -0.5 * jnp.sum(values * values, axis=0, keepdims=True)
    high = half.astype(jnp.bfloat16).astype(jnp.float32)
    rest = half - high
    middle = rest.astype(jnp.bfloat16).astype(jnp.float32)
    low = rest - middle
    width = scaled.shape[1]
    index = lax.broadcasted_iota(jnp.int32, (16, width), 0)
    first = 3 if flip else 0
    ones = 0 if flip else 3
    rows = jnp.where(index == first, high, 0.0)
    rows = jnp.where(index == first + 1, middle, rows)
    rows = jnp.where(index == first + 2, low, rows)
    rows = jnp.where((index >= ones) & (index < ones + 3), 1.0, rows)
    return rows.astype(jnp.bfloat16)


def kernel(
    points_ref, lengths_ref, noise_ref, solution_ref, residual_ref, direction_ref,
    new_solution_ref, new_residual_ref, new_direction_ref,
    blocks, line, weights, total, parts, sums_line, sums_plane, own_sums, line_sums,
    plane_send, plane_recv, pair_send, pair_recv, line_send, line_recv,
    part_send, part_recv, sl_send, sl_recv, sp_send, sp_recv,
):
    width = points_ref.shape[1]
    row, col = lax.axis_index("row"), lax.axis_index("col")
    core = lax.rem(row, 2)
    chip = row // 2
    y, z = chip // SIDE, lax.rem(chip, SIDE)
    order = plane_order()

    def at(dy, dz, dcore, dx):
        ny, nz = lax.rem(y + dy, SIDE), lax.rem(z + dz, SIDE)
        ncore = lax.rem(core + dcore, 2)
        return ((ny * SIDE + nz) * 2 + ncore, lax.rem(col + dx, SIDE))

    plane = [at(dy, dz, 0, 0) for dy, dz in order[1:]]
    others = [(q, c) for c in range(2) for q in range(SIDE)][1:]
    row_line = [at(0, 0, c, q) for q, c in others]
    sibling = at(0, 0, 1, 0)

    barrier = pltpu.get_barrier_semaphore()
    for device in plane + row_line:
        pl.semaphore_signal(barrier, inc=1, device_id=device, device_id_type=MESH)

    diagonal = lax.broadcasted_iota(jnp.int32, (FEAT, FEAT), 0) == lax.broadcasted_iota(
        jnp.int32, (FEAT, FEAT), 1
    )
    lengths = jnp.sum(jnp.where(diagonal, lengths_ref[...], 0.0), axis=1, keepdims=True)
    scaled = (points_ref[...].astype(jnp.float32) / lengths).astype(jnp.bfloat16)
    blocks[0, 0:FEAT, :] = scaled
    blocks[0, FEAT:DEEP, :] = bias_rows(scaled, False)
    blocks[0, DEEP:ROWS, :] = direction_ref[...].astype(jnp.bfloat16)

    pl.semaphore_wait(barrier, len(plane) + len(row_line))

    def remote(src, dst, send, recv, device):
        return pltpu.make_async_remote_copy(
            src_ref=src, dst_ref=dst, send_sem=send, recv_sem=recv, device_id=device, device_id_type=MESH
        )

    line_copies = [
        remote(blocks.at[0, pl.ds(0, FEAT)], line.at[q - 1], line_send.at[q - 1], line_recv.at[q - 1], at(0, 0, 0, q))
        for q in range(1, SIDE)
    ]
    for copy in line_copies:
        copy.start()
    plane_copies = [
        remote(blocks.at[0], blocks.at[k + 1], plane_send.at[k], plane_recv.at[k], plane[k]) for k in range(len(plane))
    ]
    for copy in plane_copies:
        copy.start()

    def pair_copy(p):
        return remote(blocks.at[p], blocks.at[16 + p], pair_send.at[p], pair_recv.at[p], sibling)

    weights[0:FEAT, 0:width] = scaled
    weights[FEAT:DEEP, 0:width] = bias_rows(scaled, True)
    for q in range(1, SIDE):
        line_copies[q - 1].wait_recv()
        part = line[q - 1]
        weights[0:FEAT, q * width : (q + 1) * width] = part
        weights[FEAT:DEEP, q * width : (q + 1) * width] = bias_rows(part, True)

    total[...] = jnp.zeros_like(total)

    def work(k):
        cross = lax.dot_general(
            blocks[k, 0:DEEP, :], weights[...], (((0,), (0,)), ((), ())), preferred_element_type=jnp.float32
        )
        tile = jnp.exp(cross).astype(jnp.bfloat16)
        total[...] += jnp.dot(blocks[k, DEEP:ROWS, :], tile, preferred_element_type=jnp.float32)

    pair_copy(0).start()
    work(0)
    pair_copy(0).wait_recv()
    work(16)

    def step(p, carry):
        remote(
            blocks.at[0], blocks.at[p], plane_send.at[p - 1], plane_recv.at[p - 1], plane[0]
        ).wait_recv()
        pair_copy(p).start()
        work(p)
        pair_copy(p).wait_recv()
        work(16 + p)
        return carry

    lax.fori_loop(1, 16, step, 0)

    part_copies = [
        remote(
            total.at[:, pl.ds(q * width, width)], parts.at[q - 1], part_send.at[q - 1], part_recv.at[q - 1],
            at(0, 0, 0, SIDE - q),
        )
        for q in range(1, SIDE)
    ]
    for copy in part_copies:
        copy.start()
    residual, direction = residual_ref[...], direction_ref[...]
    image = total[:, 0:width] + noise_ref[...] * direction
    for q in range(1, SIDE):
        part_copies[q - 1].wait_recv()
        image = image + parts[q - 1]

    lane = lax.broadcasted_iota(jnp.int32, (RHS, 128), 1)
    packed = jnp.zeros((RHS, 128), jnp.float32)
    for n, product in enumerate((residual * residual, direction * image, residual * image, image * image)):
        packed = jnp.where(lane == n, jnp.sum(product, axis=1, keepdims=True), packed)
    own_sums[...] = packed
    sl_copies = [
        remote(own_sums, sums_line.at[n], sl_send.at[n], sl_recv.at[n], row_line[n]) for n in range(len(row_line))
    ]
    for copy in sl_copies:
        copy.start()
    for n, copy in enumerate(sl_copies):
        copy.wait_recv()
        packed = packed + sums_line[n]
    line_sums[...] = packed
    sp_copies = [
        remote(line_sums, sums_plane.at[n], sp_send.at[n], sp_recv.at[n], plane[n]) for n in range(len(plane))
    ]
    for copy in sp_copies:
        copy.start()
    for n, copy in enumerate(sp_copies):
        copy.wait_recv()
        packed = packed + sums_plane[n]

    norm_old, curvature, mixed, square = (packed[:, n : n + 1] for n in range(4))
    step_size = norm_old / curvature
    norm_new = norm_old + step_size * (step_size * square - 2.0 * mixed)
    new_residual = residual - step_size * image
    new_solution_ref[...] = solution_ref[...] + step_size * direction
    new_residual_ref[...] = new_residual
    new_direction_ref[...] = new_residual + (norm_new / norm_old) * direction

    for copy in line_copies + plane_copies + part_copies + sl_copies + sp_copies:
        copy.wait_send()
    for p in range(16):
        pair_copy(p).wait_send()


def local(points, lengths, noise_var, solution, residual, direction):
    width = points.shape[1]
    out = jax.ShapeDtypeStruct((RHS, width), jnp.float32)
    vmem = pl.BlockSpec(memory_space=pltpu.VMEM)
    dma = pltpu.SemaphoreType.DMA
    return pl.pallas_call(
        kernel,
        out_shape=(out, out, out),
        in_specs=[vmem] * 6,
        out_specs=(vmem,) * 3,
        scratch_shapes=[
            pltpu.VMEM((32, ROWS, width), jnp.bfloat16),
            pltpu.VMEM((SIDE - 1, FEAT, width), jnp.bfloat16),
            pltpu.VMEM((DEEP, SIDE * width), jnp.bfloat16),
            pltpu.VMEM((RHS, SIDE * width), jnp.float32),
            pltpu.VMEM((SIDE - 1, RHS, width), jnp.float32),
            pltpu.VMEM((7, RHS, 128), jnp.float32),
            pltpu.VMEM((15, RHS, 128), jnp.float32),
            pltpu.VMEM((RHS, 128), jnp.float32),
            pltpu.VMEM((RHS, 128), jnp.float32),
            dma((15,)), dma((15,)), dma((16,)), dma((16,)), dma((3,)), dma((3,)),
            dma((3,)), dma((3,)), dma((7,)), dma((7,)), dma((15,)), dma((15,)),
        ],
        compiler_params=pltpu.CompilerParams(
            collective_id=0, has_side_effects=True, vmem_limit_bytes=48 << 20
        ),
        name="cg_step",
    )(points, lengths.reshape(1, FEAT), noise_var.reshape(1, width), solution, residual, direction)


def solution(mesh):
    wide = P(None, ("row", "col"))
    return jax.shard_map(
        local,
        mesh=mesh,
        in_specs=(wide, P(), P(("row", "col")), wide, wide, wide),
        out_specs=(wide, wide, wide),
        check_vma=False,
    )
```

```python
import functools

import jax
import jax.numpy as jnp
from jax import lax
from jax.experimental import pallas as pl
from jax.experimental.pallas import tpu as pltpu
from jax.sharding import PartitionSpec as P

MESH = pl.DeviceIdType.MESH
FEAT = 64
RHS = 16
DEEP = FEAT + 16
ROWS = DEEP + RHS
SIDE = 4
LATE = 11


def plane_order():
    near = (0, 1, 3, 2)
    first = [(a, 0) for a in near] + [(0, b) for b in near[1:]]
    return first + [(a, b) for b in near[1:] for a in near[1:]]


def bias_rows(scaled, flip):
    values = scaled.astype(jnp.float32)
    half = -0.5 * jnp.sum(values * values, axis=0, keepdims=True)
    high = half.astype(jnp.bfloat16).astype(jnp.float32)
    rest = half - high
    middle = rest.astype(jnp.bfloat16).astype(jnp.float32)
    low = rest - middle
    width = scaled.shape[1]
    index = lax.broadcasted_iota(jnp.int32, (16, width), 0)
    first = 3 if flip else 0
    ones = 0 if flip else 3
    rows = jnp.where(index == first, high, 0.0)
    rows = jnp.where(index == first + 1, middle, rows)
    rows = jnp.where(index == first + 2, low, rows)
    rows = jnp.where((index >= ones) & (index < ones + 3), 1.0, rows)
    return rows.astype(jnp.bfloat16)


def kernel(
    points_hbm, lengths_hbm, noise_hbm, solution_hbm, residual_hbm, direction_hbm,
    new_solution_ref, new_residual_ref, new_direction_ref,
    points_ref, lengths_ref, noise_ref, solution_ref, residual_ref, direction_ref,
    blocks, line, weights, lefts, cross, tiles, total, parts, sums_line, sums_plane, own_sums, line_sums,
    in_sem, plane_send, plane_recv, pair_send, pair_recv, line_send, line_recv,
    part_send, part_recv, sl_send, sl_recv, sp_send, sp_recv,
):
    width = points_ref.shape[1]
    row, col = lax.axis_index("row"), lax.axis_index("col")
    core = lax.rem(row, 2)
    chip = row // 2
    y, z = chip // SIDE, lax.rem(chip, SIDE)
    order = plane_order()
    slot_of = {offset: n for n, offset in enumerate(order)}

    def at(first, second, dcore, dx):
        dy = first * core + second * (1 - core)
        dz = first * (1 - core) + second * core
        ny, nz = lax.rem(y + dy, SIDE), lax.rem(z + dz, SIDE)
        return ((ny * SIDE + nz) * 2 + lax.rem(core + dcore, 2), lax.rem(col + dx, SIDE))

    plane = [at(a, b, 0, 0) for a, b in order[1:]]
    others = [(q, c) for c in range(2) for q in range(SIDE)][1:]
    row_line = [at(0, 0, c, q) for q, c in others]
    sibling = at(0, 0, 1, 0)

    barrier = pltpu.get_barrier_semaphore()
    greeted = plane[:6] + row_line
    for device in greeted:
        pl.semaphore_signal(barrier, inc=1, device_id=device, device_id_type=MESH)

    pairs = (
        (points_hbm, points_ref), (lengths_hbm, lengths_ref), (direction_hbm, direction_ref),
        (noise_hbm, noise_ref), (solution_hbm, solution_ref), (residual_hbm, residual_ref),
    )
    loads = [pltpu.make_async_copy(src, dst, in_sem.at[n]) for n, (src, dst) in enumerate(pairs)]
    for copy in loads:
        copy.start()
    total[...] = jnp.zeros_like(total)
    cross[1] = jnp.full(cross.shape[1:], -1e4, jnp.float32)
    tiles[0] = jnp.zeros(tiles.shape[1:], jnp.bfloat16)
    for copy in loads[:3]:
        copy.wait()

    diagonal = lax.broadcasted_iota(jnp.int32, (FEAT, FEAT), 0) == lax.broadcasted_iota(
        jnp.int32, (FEAT, FEAT), 1
    )
    lengths = jnp.sum(jnp.where(diagonal, lengths_ref[...], 0.0), axis=1, keepdims=True)
    scaled = (points_ref[...].astype(jnp.float32) / lengths).astype(jnp.bfloat16)
    blocks[0, 0:FEAT, :] = scaled
    blocks[0, FEAT:DEEP, :] = bias_rows(scaled, False)
    blocks[0, DEEP:ROWS, :] = direction_ref[...].astype(jnp.bfloat16)

    pl.semaphore_wait(barrier, len(greeted))

    def remote(src, dst, send, recv, device):
        return pltpu.make_async_remote_copy(
            src_ref=src, dst_ref=dst, send_sem=send, recv_sem=recv, device_id=device, device_id_type=MESH
        )

    def plane_copy(src, dst, device):
        return remote(blocks.at[src], blocks.at[dst], plane_send.at[dst - 1], plane_recv.at[dst - 1], device)

    def pair_copy(p):
        return remote(blocks.at[p], blocks.at[16 + p], pair_send.at[p], pair_recv.at[p], sibling)

    line_copies = [
        remote(blocks.at[0, pl.ds(0, FEAT)], line.at[q - 1], line_send.at[q - 1], line_recv.at[q - 1], at(0, 0, 0, q))
        for q in (1, 3, 2)
    ]
    plane_copies = [plane_copy(0, k, plane[k - 1]) for k in range(1, 7)]
    pair_copy(0).start()
    for copy in line_copies[:2] + plane_copies[:2] + line_copies[2:] + plane_copies[2:]:
        copy.start()

    def transpose(block):
        lefts[block, :, 0:DEEP] = blocks[block, 0:DEEP, :].T

    weights[0:FEAT, 0:width] = scaled
    weights[FEAT:DEEP, 0:width] = bias_rows(scaled, True)
    transpose(0)
    for copy, q in zip(line_copies, (1, 3, 2)):
        copy.wait_recv()
        part = line[q - 1]
        weights[0:FEAT, q * width : (q + 1) * width] = part
        weights[FEAT:DEEP, q * width : (q + 1) * width] = bias_rows(part, True)

    for k in range(1, 4):
        plane_copies[k - 1].wait_recv()
        first = order[k][0]
        for second in (1, 3, 2):
            copy = plane_copy(k, slot_of[first, second], at(0, second, 0, 0))
            copy.start()
            plane_copies.append(copy)

    def cross_stage(block, q, slot):
        cross[slot] = jnp.dot(
            lefts[block, :, 0:DEEP], weights[:, q * width : (q + 1) * width], preferred_element_type=jnp.float32
        )

    def exp_stage(slot):
        tiles[slot] = jnp.exp(cross[slot]).astype(jnp.bfloat16)

    def sum_stage(block, q, slot):
        total[:, q * width : (q + 1) * width] += jnp.dot(
            blocks[block, DEEP:ROWS, :], tiles[slot], preferred_element_type=jnp.float32
        )

    def body(parts_done, p, carry):
        before = jnp.maximum(p - 1, 0)
        after = jnp.minimum(p + 1, 15)

        @pl.when((p < 15) & (p > 2))
        def _():
            remote(
                blocks.at[0], blocks.at[after], plane_send.at[after - 1], plane_recv.at[after - 1], plane[0]
            ).wait_recv()

        @pl.when(p < 15)
        def _():
            pair_copy(after).start()

        pair_copy(p).wait_recv()
        transpose(16 + p)
        chunks = [(16 * half + p, q) for half in range(2) for q in range(SIDE) if q or not parts_done]
        lagged = [(16 + before, 2), (16 + before, 3)] + chunks
        for c, (block, q) in enumerate(chunks):
            sum_stage(*lagged[c], c % 2)
            exp_stage((c + 1) % 2)
            cross_stage(block, q, c % 2)
            if c == len(chunks) // 2 - 1:
                transpose(after)
        return carry

    lax.fori_loop(0, 16 - LATE, functools.partial(body, False), 0)
    lax.fori_loop(16 - LATE, 16, functools.partial(body, True), 0)

    def late(n):
        return 16 * lax.rem(n, 2) + 16 - LATE + n // 2

    sum_stage(31, 2, 0)
    exp_stage(1)
    cross_stage(late(0), 0, 0)
    sum_stage(31, 3, 1)
    exp_stage(0)
    cross_stage(late(1), 0, 1)
    part_copies = [
        remote(
            total.at[:, pl.ds(q * width, width)], parts.at[q - 1], part_send.at[q - 1], part_recv.at[q - 1],
            at(0, 0, 0, SIDE - q),
        )
        for q in (1, 3, 2)
    ]
    for copy in part_copies:
        copy.start()

    def own(m, carry):
        for c in range(6):
            n = 6 * m + 2 + c
            sum_stage(late(n - 2), 0, c % 2)
            exp_stage((c + 1) % 2)
            cross_stage(late(n), 0, c % 2)
        return carry

    lax.fori_loop(0, (2 * LATE - 4) // 6, own, 0)
    for n in (2 * LATE - 2, 2 * LATE - 1):
        sum_stage(late(n - 2), 0, n % 2)
        exp_stage((n + 1) % 2)
        cross_stage(late(n), 0, n % 2)
    sum_stage(late(2 * LATE - 2), 0, 0)
    exp_stage(1)
    sum_stage(late(2 * LATE - 1), 0, 1)
    for copy in loads[3:]:
        copy.wait()
    residual, direction = residual_ref[...], direction_ref[...]
    image = total[:, 0:width] + noise_ref[...] * direction
    for copy, q in zip(part_copies, (1, 3, 2)):
        copy.wait_recv()
        image = image + parts[q - 1]

    lane = lax.broadcasted_iota(jnp.int32, (RHS, 128), 1)
    packed = jnp.zeros((RHS, 128), jnp.float32)
    for n, product in enumerate((residual * residual, direction * image, residual * image, image * image)):
        packed = jnp.where(lane == n, jnp.sum(product, axis=1, keepdims=True), packed)
    own_sums[...] = packed
    sl_copies = [
        remote(own_sums, sums_line.at[n], sl_send.at[n], sl_recv.at[n], row_line[n]) for n in range(len(row_line))
    ]
    for copy in sl_copies:
        copy.start()
    for n, copy in enumerate(sl_copies):
        copy.wait_recv()
        packed = packed + sums_line[n]
    line_sums[...] = packed
    sp_copies = [
        remote(line_sums, sums_plane.at[n], sp_send.at[n], sp_recv.at[n], plane[n]) for n in range(len(plane))
    ]
    for copy in sp_copies:
        copy.start()
    for n, copy in enumerate(sp_copies):
        copy.wait_recv()
        packed = packed + sums_plane[n]

    norm_old, curvature, mixed, square = (packed[:, n : n + 1] for n in range(4))
    step_size = norm_old / curvature
    norm_new = norm_old + step_size * (step_size * square - 2.0 * mixed)
    new_residual = residual - step_size * image
    new_solution_ref[...] = solution_ref[...] + step_size * direction
    new_residual_ref[...] = new_residual
    new_direction_ref[...] = new_residual + (norm_new / norm_old) * direction

    for copy in line_copies + plane_copies + part_copies + sl_copies + sp_copies:
        copy.wait_send()
    for p in range(16):
        pair_copy(p).wait_send()


def local(points, lengths, noise_var, solution, residual, direction):
    width = points.shape[1]
    out = jax.ShapeDtypeStruct((RHS, width), jnp.float32)
    vmem, dma = pltpu.VMEM, pltpu.SemaphoreType.DMA
    wide = vmem((RHS, width), jnp.float32)
    return pl.pallas_call(
        kernel,
        out_shape=(out, out, out),
        in_specs=[pl.BlockSpec(memory_space=pl.ANY)] * 6,
        out_specs=(pl.BlockSpec(memory_space=vmem),) * 3,
        scratch_shapes=[
            vmem((FEAT, width), jnp.bfloat16),
            vmem((1, FEAT), jnp.float32),
            vmem((1, width), jnp.float32),
            wide,
            wide,
            wide,
            vmem((32, ROWS, width), jnp.bfloat16),
            vmem((SIDE - 1, FEAT, width), jnp.bfloat16),
            vmem((DEEP, SIDE * width), jnp.bfloat16),
            vmem((32, width, 128), jnp.bfloat16),
            vmem((2, width, width), jnp.float32),
            vmem((2, width, width), jnp.bfloat16),
            vmem((RHS, SIDE * width), jnp.float32),
            vmem((SIDE - 1, RHS, width), jnp.float32),
            vmem((7, RHS, 128), jnp.float32),
            vmem((15, RHS, 128), jnp.float32),
            vmem((RHS, 128), jnp.float32),
            vmem((RHS, 128), jnp.float32),
            dma((6,)), dma((15,)), dma((15,)), dma((16,)), dma((16,)), dma((3,)), dma((3,)),
            dma((3,)), dma((3,)), dma((7,)), dma((7,)), dma((15,)), dma((15,)),
        ],
        compiler_params=pltpu.CompilerParams(
            collective_id=0, has_side_effects=True, vmem_limit_bytes=63 << 20
        ),
        name="cg_step",
    )(points, lengths.reshape(1, FEAT), noise_var.reshape(1, width), solution, residual, direction)


def solution(mesh):
    wide = P(None, ("row", "col"))
    return jax.shard_map(
        local,
        mesh=mesh,
        in_specs=(wide, P(), P(("row", "col")), wide, wide, wide),
        out_specs=(wide, wide, wide),
        check_vma=False,
    )
```

```python
import functools

import jax
import jax.numpy as jnp
from jax import lax
from jax.experimental import pallas as pl
from jax.experimental.pallas import tpu as pltpu
from jax.sharding import PartitionSpec as P

MESH = pl.DeviceIdType.MESH
FEAT = 64
RHS = 16
DEEP = FEAT + 16
ROWS = DEEP + RHS
SIDE = 4
LATE = 11

ORDER = (
    (0, 0), (1, 0), (3, 0), (0, 1), (0, 3), (2, 0), (1, 1), (1, 3),
    (3, 1), (3, 3), (0, 2), (1, 2), (3, 2), (2, 1), (2, 3), (2, 2),
)
SLOT = {offset: n for n, offset in enumerate(ORDER)}
WAVES = (
    [((0, 0), step, step, None) for step in ((1, 0), (3, 0), (0, 1), (0, 3))],
    [
        ((1, 0), (0, 1), (1, 1), None), ((3, 0), (0, 1), (3, 1), None),
        ((1, 0), (0, 3), (1, 3), None), ((3, 0), (0, 3), (3, 3), None),
        ((1, 0), (1, 0), (2, 0), 0), ((3, 0), (3, 0), (2, 0), 1),
        ((0, 1), (0, 1), (0, 2), 0), ((0, 3), (0, 3), (0, 2), 1),
    ],
    [
        ((2, 0), (0, 1), (2, 1), None), ((2, 0), (0, 3), (2, 3), None),
        ((1, 1), (0, 1), (1, 2), 0), ((1, 3), (0, 3), (1, 2), 1),
        ((3, 1), (0, 1), (3, 2), 0), ((3, 3), (0, 3), (3, 2), 1),
    ],
    [((2, 1), (0, 1), (2, 2), 0), ((2, 3), (0, 3), (2, 2), 1)],
)


def bias_rows(scaled, flip):
    values = scaled.astype(jnp.float32)
    half = -0.5 * jnp.sum(values * values, axis=0, keepdims=True)
    high = half.astype(jnp.bfloat16).astype(jnp.float32)
    rest = half - high
    middle = rest.astype(jnp.bfloat16).astype(jnp.float32)
    low = rest - middle
    width = scaled.shape[1]
    index = lax.broadcasted_iota(jnp.int32, (16, width), 0)
    first = 3 if flip else 0
    ones = 0 if flip else 3
    rows = jnp.where(index == first, high, 0.0)
    rows = jnp.where(index == first + 1, middle, rows)
    rows = jnp.where(index == first + 2, low, rows)
    rows = jnp.where((index >= ones) & (index < ones + 3), 1.0, rows)
    return rows.astype(jnp.bfloat16)


def kernel(
    points_hbm, lengths_hbm, noise_hbm, residual_hbm, direction_hbm,
    image_ref, step_ref, growth_ref,
    points_ref, lengths_ref, noise_ref, residual_ref, direction_ref,
    blocks, line, weights, lefts, cross, tiles, total, parts, sums_line, sums_plane, own_sums, line_sums,
    in_sem, plane_send, plane_recv, pair_send, pair_recv, line_send, line_recv,
    part_send, part_recv, sl_send, sl_recv, sp_send, sp_recv,
):
    width = points_ref.shape[1]
    row, col = lax.axis_index("row"), lax.axis_index("col")
    core = lax.rem(row, 2)
    chip = row // 2
    y, z = chip // SIDE, lax.rem(chip, SIDE)

    def at(first, second, dcore, dx):
        dy = first * core + second * (1 - core)
        dz = first * (1 - core) + second * core
        ny, nz = lax.rem(y + dy, SIDE), lax.rem(z + dz, SIDE)
        return ((ny * SIDE + nz) * 2 + lax.rem(core + dcore, 2), lax.rem(col + dx, SIDE))

    plane = [at(a, b, 0, 0) for a, b in ORDER[1:]]
    others = [(q, c) for c in range(2) for q in range(SIDE)][1:]
    row_line = [at(0, 0, c, q) for q, c in others]
    sibling = at(0, 0, 1, 0)

    barrier = pltpu.get_barrier_semaphore()
    greeted = plane[:4] + [at(0, 0, 0, 1), at(0, 0, 0, 3), sibling]
    for device in greeted:
        pl.semaphore_signal(barrier, inc=1, device_id=device, device_id_type=MESH)

    pairs = (
        (points_hbm, points_ref), (lengths_hbm, lengths_ref), (direction_hbm, direction_ref),
        (noise_hbm, noise_ref), (residual_hbm, residual_ref),
    )
    loads = [pltpu.make_async_copy(src, dst, in_sem.at[n]) for n, (src, dst) in enumerate(pairs)]
    for copy in loads:
        copy.start()
    total[...] = jnp.zeros_like(total)
    cross[1] = jnp.full(cross.shape[1:], -1e4, jnp.float32)
    tiles[0] = jnp.zeros(tiles.shape[1:], jnp.bfloat16)
    for copy in loads[:3]:
        copy.wait()

    diagonal = lax.broadcasted_iota(jnp.int32, (FEAT, FEAT), 0) == lax.broadcasted_iota(
        jnp.int32, (FEAT, FEAT), 1
    )
    lengths = jnp.sum(jnp.where(diagonal, lengths_ref[...], 0.0), axis=1, keepdims=True)
    scaled = (points_ref[...].astype(jnp.float32) / lengths).astype(jnp.bfloat16)
    blocks[0, 0:FEAT, :] = scaled
    blocks[0, FEAT:DEEP, :] = bias_rows(scaled, False)
    blocks[0, DEEP:ROWS, :] = direction_ref[...].astype(jnp.bfloat16)

    pl.semaphore_wait(barrier, len(greeted))

    def remote(src, dst, send, recv, device):
        return pltpu.make_async_remote_copy(
            src_ref=src, dst_ref=dst, send_sem=send, recv_sem=recv, device_id=device, device_id_type=MESH
        )

    def plane_copy(src, step, dst, half):
        rows = pl.ds(0, ROWS) if half is None else pl.ds(half * (ROWS // 2), ROWS // 2)
        return remote(
            blocks.at[SLOT[src], rows], blocks.at[SLOT[dst], rows], plane_send.at[SLOT[dst], half or 0],
            plane_recv.at[SLOT[dst], half or 0], at(*step, 0, 0),
        )

    waves = [[plane_copy(*entry) for entry in wave] for wave in WAVES]

    def pair_copy(p):
        return remote(blocks.at[p], blocks.at[16 + p], pair_send.at[p], pair_recv.at[p], sibling)

    def next_wave(n):
        for copy in waves[n]:
            copy.wait_recv()
        if n + 1 < len(waves):
            for copy in waves[n + 1]:
                copy.start()
        for slot in sorted({SLOT[entry[2]] for entry in WAVES[n]}):
            pair_copy(slot).start()

    line_near = [
        remote(blocks.at[0, pl.ds(0, FEAT)], line.at[q - 1], line_send.at[n], line_recv.at[n], at(0, 0, 0, q))
        for n, q in enumerate((1, 3))
    ]
    line_far = [
        remote(
            line.at[q - 1, pl.ds(n * (FEAT // 2), FEAT // 2)], line.at[1, pl.ds(n * (FEAT // 2), FEAT // 2)],
            line_send.at[2 + n], line_recv.at[2 + n], at(0, 0, 0, q),
        )
        for n, q in enumerate((1, 3))
    ]
    pair_copy(0).start()
    for copy in line_near + waves[0]:
        copy.start()

    def transpose(block):
        lefts[block, :, 0:DEEP] = blocks[block, 0:DEEP, :].T

    def set_rows(q, part):
        weights[0:FEAT, q * width : (q + 1) * width] = part
        weights[FEAT:DEEP, q * width : (q + 1) * width] = bias_rows(part, True)

    def cross_stage(block, q, slot):
        cross[slot] = jnp.dot(
            lefts[block, :, 0:DEEP], weights[:, q * width : (q + 1) * width], preferred_element_type=jnp.float32
        )

    def exp_stage(slot):
        tiles[slot] = jnp.exp(cross[slot]).astype(jnp.bfloat16)

    def sum_stage(block, q, slot):
        columns = pl.ds(pl.multiple_of(q * width, width), width)
        total[:, columns] += jnp.dot(
            blocks[block, DEEP:ROWS, :], tiles[slot], preferred_element_type=jnp.float32
        )

    def run(chunks, before, middle=None):
        lagged = before + chunks
        for c, (block, q) in enumerate(chunks):
            sum_stage(*lagged[c], c % 2)
            exp_stage((c + 1) % 2)
            cross_stage(block, q, c % 2)
            if middle is not None and c == len(chunks) // 2 - 1:
                middle()
        return chunks[-2:]

    def loop(first, last, chunks_of, before, top=None, middle=None):
        def body(p, carry):
            if top is not None:
                top(p)
            own = chunks_of(p - 1)[-2:]
            lag = [
                (jnp.where(p == first, old[0], new[0]), jnp.where(p == first, old[1], new[1]))
                for old, new in zip(before, own)
            ]
            run(chunks_of(p), lag, None if middle is None else functools.partial(middle, p))
            return carry

        lax.fori_loop(first, last, body, 0)
        return chunks_of(last - 1)[-2:]

    def both(p, parts_):
        return [(block, q) for block in (p, 16 + p) for q in parts_]

    set_rows(0, scaled)
    transpose(0)
    pair_copy(0).wait_recv()
    transpose(16)
    lag = run([(0, 0), (16, 0)], [(0, 0), (0, 0)])
    for near, far in zip(line_near, line_far):
        near.wait_recv()
        far.start()
    set_rows(1, line[0])
    set_rows(3, line[2])
    lag = run([(0, 1), (16, 1), (0, 3), (16, 3)], lag)
    next_wave(0)
    transpose(1)

    def pair_arrives(p):
        pair_copy(p).wait_recv()
        transpose(16 + p)

    lag = loop(
        1, 5, lambda p: both(p, (0, 1, 3)), lag, pair_arrives, lambda p: transpose(jnp.minimum(p + 1, 4))
    )
    for copy in line_far:
        copy.wait_recv()
    set_rows(2, line[1])
    lag = loop(0, 5, lambda p: both(p, (2,)), lag)
    next_wave(1)
    transpose(5)

    def arrives(p):
        pl.when(p == 9)(functools.partial(next_wave, 2))
        pl.when(p == 13)(functools.partial(next_wave, 3))
        pair_arrives(p)

    lag = loop(5, 16, lambda p: both(p, (1, 2, 3)), lag, arrives, lambda p: transpose(jnp.minimum(p + 1, 15)))

    def late(n):
        return (16 * lax.rem(n, 2) + 16 - LATE + n // 2, 0)

    lag = run([late(0), late(1)], lag)
    part_copies = [
        remote(
            total.at[:, pl.ds(q * width, width)], parts.at[q - 1], part_send.at[q - 1], part_recv.at[q - 1],
            at(0, 0, 0, SIDE - q),
        )
        for q in (1, 3, 2)
    ]
    for copy in part_copies:
        copy.start()
    rounds = (2 * LATE - 4) // 6
    lag = loop(0, rounds, lambda m: [late(6 * m + 2 + c) for c in range(6)], lag)
    lag = run([late(2 * LATE - 2), late(2 * LATE - 1)], lag)
    sum_stage(*lag[0], 0)
    exp_stage(1)
    sum_stage(*lag[1], 1)
    for copy in loads[3:]:
        copy.wait()
    residual, direction = residual_ref[...], direction_ref[...]
    image = total[:, 0:width] + noise_ref[...] * direction
    for copy, q in zip(part_copies, (1, 3, 2)):
        copy.wait_recv()
        image = image + parts[q - 1]

    image_ref[...] = image
    lane = lax.broadcasted_iota(jnp.int32, (RHS, 128), 1)
    side = lax.broadcasted_iota(jnp.int32, (RHS, 128), 0)
    packed = jnp.zeros((RHS, 128), jnp.float32)
    for n, product in enumerate((residual * residual, direction * image, residual * image, image * image)):
        packed = jnp.where(lane == RHS * n + side, jnp.sum(product, axis=1, keepdims=True), packed)
    own_sums[...] = jnp.sum(packed, axis=0, keepdims=True)
    sl_copies = [
        remote(own_sums, sums_line.at[n], sl_send.at[n], sl_recv.at[n], row_line[n]) for n in range(len(row_line))
    ]
    for copy in sl_copies:
        copy.start()
    for copy in sl_copies:
        copy.wait_recv()
    line_sums[...] = own_sums[...] + jnp.sum(sums_line[...], axis=0)
    sp_copies = [
        remote(line_sums, sums_plane.at[n], sp_send.at[n], sp_recv.at[n], plane[n]) for n in range(len(plane))
    ]
    for copy in sp_copies:
        copy.start()
    for copy in sp_copies:
        copy.wait_recv()
    packed = line_sums[...] + jnp.sum(sums_plane[...], axis=0)

    norm_old, curvature, mixed, square = (
        jnp.sum(jnp.where(lane == RHS * n + side, packed, 0.0), axis=1, keepdims=True) for n in range(4)
    )
    step_size = norm_old / curvature
    norm_new = norm_old + step_size * (step_size * square - 2.0 * mixed)
    step_ref[...] = jnp.broadcast_to(step_size, step_ref.shape)
    growth_ref[...] = jnp.broadcast_to(norm_new / norm_old, growth_ref.shape)

    for copy in line_near + line_far + sum(waves, []) + part_copies + sl_copies + sp_copies:
        copy.wait_send()
    for p in range(16):
        pair_copy(p).wait_send()


def local(points, lengths, noise_var, solution, residual, direction):
    width = points.shape[1]
    out = jax.ShapeDtypeStruct((RHS, width), jnp.float32)
    vmem, dma = pltpu.VMEM, pltpu.SemaphoreType.DMA
    wide = vmem((RHS, width), jnp.float32)
    image, step_size, growth = pl.pallas_call(
        kernel,
        out_shape=(out, out, out),
        in_specs=[pl.BlockSpec(memory_space=pl.ANY)] * 5,
        out_specs=(pl.BlockSpec(memory_space=vmem),) * 3,
        scratch_shapes=[
            vmem((FEAT, width), jnp.bfloat16),
            vmem((1, FEAT), jnp.float32),
            vmem((1, width), jnp.float32),
            wide,
            wide,
            vmem((32, ROWS, width), jnp.bfloat16),
            vmem((SIDE - 1, FEAT, width), jnp.bfloat16),
            vmem((DEEP, SIDE * width), jnp.bfloat16),
            vmem((32, width, 128), jnp.bfloat16),
            vmem((2, width, width), jnp.float32),
            vmem((2, width, width), jnp.bfloat16),
            vmem((RHS, SIDE * width), jnp.float32),
            vmem((SIDE - 1, RHS, width), jnp.float32),
            vmem((7, 1, 128), jnp.float32),
            vmem((15, 1, 128), jnp.float32),
            vmem((1, 128), jnp.float32),
            vmem((1, 128), jnp.float32),
            dma((5,)), dma((16, 2)), dma((16, 2)), dma((16,)), dma((16,)), dma((4,)), dma((4,)),
            dma((3,)), dma((3,)), dma((7,)), dma((7,)), dma((15,)), dma((15,)),
        ],
        compiler_params=pltpu.CompilerParams(
            collective_id=0, has_side_effects=True, vmem_limit_bytes=63 << 20
        ),
        name="cg_step",
    )(points, lengths.reshape(1, FEAT), noise_var.reshape(1, width), residual, direction)
    new_residual = residual - step_size * image
    return solution + step_size * direction, new_residual, new_residual + growth * direction


def solution(mesh):
    wide = P(None, ("row", "col"))
    return jax.shard_map(
        local,
        mesh=mesh,
        in_specs=(wide, P(), P(("row", "col")), wide, wide, wide),
        out_specs=(wide, wide, wide),
        check_vma=False,
    )
```

```python
import functools

import jax
import jax.numpy as jnp
from jax import lax
from jax.experimental import pallas as pl
from jax.experimental.pallas import tpu as pltpu
from jax.sharding import PartitionSpec as P

MESH = pl.DeviceIdType.MESH
FEAT = 64
RHS = 16
DEEP = FEAT + 16
ROWS = DEEP + RHS
SIDE = 4
LATE = 11

ORDER = (
    (0, 0), (1, 0), (3, 0), (0, 1), (0, 3), (2, 0), (1, 1), (1, 3),
    (3, 1), (3, 3), (0, 2), (1, 2), (3, 2), (2, 1), (2, 3), (2, 2),
)
SLOT = {offset: n for n, offset in enumerate(ORDER)}
WAVES = (
    [((0, 0), step, step, None) for step in ((1, 0), (3, 0), (0, 1), (0, 3))],
    [
        ((1, 0), (0, 1), (1, 1), None), ((3, 0), (0, 1), (3, 1), None),
        ((1, 0), (0, 3), (1, 3), None), ((3, 0), (0, 3), (3, 3), None),
        ((1, 0), (1, 0), (2, 0), 0), ((3, 0), (3, 0), (2, 0), 1),
        ((0, 1), (0, 1), (0, 2), 0), ((0, 3), (0, 3), (0, 2), 1),
    ],
    [
        ((2, 0), (0, 1), (2, 1), None), ((2, 0), (0, 3), (2, 3), None),
        ((1, 1), (0, 1), (1, 2), 0), ((1, 3), (0, 3), (1, 2), 1),
        ((3, 1), (0, 1), (3, 2), 0), ((3, 3), (0, 3), (3, 2), 1),
    ],
    [((2, 1), (0, 1), (2, 2), 0), ((2, 3), (0, 3), (2, 2), 1)],
)


def bias_rows(scaled, flip):
    values = scaled.astype(jnp.float32)
    half = -0.5 * jnp.sum(values * values, axis=0, keepdims=True)
    high = half.astype(jnp.bfloat16).astype(jnp.float32)
    rest = half - high
    middle = rest.astype(jnp.bfloat16).astype(jnp.float32)
    low = rest - middle
    width = scaled.shape[1]
    index = lax.broadcasted_iota(jnp.int32, (16, width), 0)
    first = 3 if flip else 0
    ones = 0 if flip else 3
    rows = jnp.where(index == first, high, 0.0)
    rows = jnp.where(index == first + 1, middle, rows)
    rows = jnp.where(index == first + 2, low, rows)
    rows = jnp.where((index >= ones) & (index < ones + 3), 1.0, rows)
    return rows.astype(jnp.bfloat16)


def kernel(
    points_hbm, lengths_hbm, noise_hbm, residual_hbm, direction_hbm,
    image_hbm, step_ref, growth_ref,
    image_ref, points_ref, lengths_ref, noise_ref, residual_ref, direction_ref,
    blocks, line, weights, lefts, cross, tiles, total, parts, sums_line, sums_plane, own_sums, line_sums,
    in_sem, plane_send, plane_recv, pair_send, pair_recv, line_send, line_recv,
    part_send, part_recv, sl_send, sl_recv, sp_send, sp_recv,
):
    width = points_ref.shape[1]
    row, col = lax.axis_index("row"), lax.axis_index("col")
    core = lax.rem(row, 2)
    chip = row // 2
    y, z = chip // SIDE, lax.rem(chip, SIDE)

    def at(first, second, dcore, dx):
        dy = first * core + second * (1 - core)
        dz = first * (1 - core) + second * core
        ny, nz = lax.rem(y + dy, SIDE), lax.rem(z + dz, SIDE)
        return ((ny * SIDE + nz) * 2 + lax.rem(core + dcore, 2), lax.rem(col + dx, SIDE))

    plane = [at(a, b, 0, 0) for a, b in ORDER[1:]]
    others = [(q, c) for c in range(2) for q in range(SIDE)][1:]
    row_line = [at(0, 0, c, q) for q, c in others]
    sibling = at(0, 0, 1, 0)

    barrier = pltpu.get_barrier_semaphore()
    greeted = plane[:4] + [at(0, 0, 0, 1), at(0, 0, 0, 3), sibling]
    for device in greeted:
        pl.semaphore_signal(barrier, inc=1, device_id=device, device_id_type=MESH)

    pairs = (
        (points_hbm, points_ref), (lengths_hbm, lengths_ref), (direction_hbm, direction_ref),
        (noise_hbm, noise_ref), (residual_hbm, residual_ref),
    )
    loads = [pltpu.make_async_copy(src, dst, in_sem.at[n]) for n, (src, dst) in enumerate(pairs)]
    for copy in loads:
        copy.start()
    total[...] = jnp.zeros_like(total)
    cross[1] = jnp.full(cross.shape[1:], -1e4, jnp.float32)
    tiles[0] = jnp.zeros(tiles.shape[1:], jnp.bfloat16)
    for copy in loads[:3]:
        copy.wait()

    diagonal = lax.broadcasted_iota(jnp.int32, (FEAT, FEAT), 0) == lax.broadcasted_iota(
        jnp.int32, (FEAT, FEAT), 1
    )
    lengths = jnp.sum(jnp.where(diagonal, lengths_ref[...], 0.0), axis=1, keepdims=True)
    scaled = (points_ref[...].astype(jnp.float32) / lengths).astype(jnp.bfloat16)
    blocks[0, 0:FEAT, :] = scaled
    blocks[0, FEAT:DEEP, :] = bias_rows(scaled, False)
    blocks[0, DEEP:ROWS, :] = direction_ref[...].astype(jnp.bfloat16)

    pl.semaphore_wait(barrier, len(greeted))

    def remote(src, dst, send, recv, device):
        return pltpu.make_async_remote_copy(
            src_ref=src, dst_ref=dst, send_sem=send, recv_sem=recv, device_id=device, device_id_type=MESH
        )

    def plane_copy(src, step, dst, half):
        rows = pl.ds(0, ROWS) if half is None else pl.ds(half * (ROWS // 2), ROWS // 2)
        return remote(
            blocks.at[SLOT[src], rows], blocks.at[SLOT[dst], rows], plane_send.at[SLOT[dst], half or 0],
            plane_recv.at[SLOT[dst], half or 0], at(*step, 0, 0),
        )

    waves = [[plane_copy(*entry) for entry in wave] for wave in WAVES]

    def pair_copy(p):
        return remote(blocks.at[p], blocks.at[16 + p], pair_send.at[p], pair_recv.at[p], sibling)

    def next_wave(n):
        for copy in waves[n]:
            copy.wait_recv()
        if n + 1 < len(waves):
            for copy in waves[n + 1]:
                copy.start()
        for slot in sorted({SLOT[entry[2]] for entry in WAVES[n]}):
            pair_copy(slot).start()

    line_near = [
        remote(blocks.at[0, pl.ds(0, FEAT)], line.at[q - 1], line_send.at[n], line_recv.at[n], at(0, 0, 0, q))
        for n, q in enumerate((1, 3))
    ]
    line_far = [
        remote(
            line.at[q - 1, pl.ds(n * (FEAT // 2), FEAT // 2)], line.at[1, pl.ds(n * (FEAT // 2), FEAT // 2)],
            line_send.at[2 + n], line_recv.at[2 + n], at(0, 0, 0, q),
        )
        for n, q in enumerate((1, 3))
    ]
    pair_copy(0).start()
    for copy in line_near + waves[0]:
        copy.start()

    def transpose(block):
        lefts[block, :, 0:DEEP] = blocks[block, 0:DEEP, :].T

    def set_rows(q, part):
        weights[0:FEAT, q * width : (q + 1) * width] = part
        weights[FEAT:DEEP, q * width : (q + 1) * width] = bias_rows(part, True)

    def cross_stage(block, q, slot):
        cross[slot] = jnp.dot(
            lefts[block, :, 0:DEEP], weights[:, q * width : (q + 1) * width], preferred_element_type=jnp.float32
        )

    def exp_stage(slot):
        tiles[slot] = jnp.exp(cross[slot]).astype(jnp.bfloat16)

    def sum_stage(block, q, slot):
        columns = pl.ds(pl.multiple_of(q * width, width), width)
        total[:, columns] += jnp.dot(
            blocks[block, DEEP:ROWS, :], tiles[slot], preferred_element_type=jnp.float32
        )

    def run(chunks, before, middle=None):
        lagged = before + chunks
        for c, (block, q) in enumerate(chunks):
            sum_stage(*lagged[c], c % 2)
            exp_stage((c + 1) % 2)
            cross_stage(block, q, c % 2)
            if middle is not None and c == len(chunks) // 2 - 1:
                middle()
        return chunks[-2:]

    def loop(first, last, step, chunks_of, before, top=None, middle=None):
        def body(n, carry):
            p = first + step * n
            if top is not None:
                top(p)
            own = chunks_of(p - step)[-2:]
            lag = [
                (jnp.where(n == 0, old[0], new[0]), jnp.where(n == 0, old[1], new[1]))
                for old, new in zip(before, own)
            ]
            run(chunks_of(p), lag, None if middle is None else functools.partial(middle, p))
            return carry

        lax.fori_loop(0, (last - first) // step, body, 0)
        return chunks_of(last - step)[-2:]

    def both(p, parts_):
        return [(block, q) for block in (p, 16 + p) for q in parts_]

    set_rows(0, scaled)
    transpose(0)
    pair_copy(0).wait_recv()
    transpose(16)
    lag = run([(0, 0), (16, 0)], [(0, 0), (0, 0)])
    for near, far in zip(line_near, line_far):
        near.wait_recv()
        far.start()
    set_rows(1, line[0])
    set_rows(3, line[2])
    lag = run([(0, 1), (16, 1), (0, 3), (16, 3)], lag)
    next_wave(0)
    transpose(1)
    transpose(2)

    def pair_arrives(p):
        pair_copy(p).wait_recv()
        transpose(16 + p)

    def two_arrive(p):
        pair_arrives(p)
        pair_arrives(p + 1)

    def two(p, parts_):
        return both(p, parts_) + both(p + 1, parts_)

    def two_follow(last, p):
        transpose(jnp.minimum(p + 2, last))
        transpose(jnp.minimum(p + 3, last))

    lag = loop(
        1, 5, 2, lambda p: two(p, (0, 1, 3)), lag, two_arrive, functools.partial(two_follow, 4)
    )
    for copy in line_far:
        copy.wait_recv()
    set_rows(2, line[1])
    lag = run([chunk for p in range(5) for chunk in both(p, (2,))], lag)
    next_wave(1)
    transpose(5)
    transpose(6)

    def arrives(p):
        pl.when(p == 9)(functools.partial(next_wave, 2))
        pl.when(p == 13)(functools.partial(next_wave, 3))
        two_arrive(p)

    lag = loop(5, 15, 2, lambda p: two(p, (1, 2, 3)), lag, arrives, functools.partial(two_follow, 15))
    pair_arrives(15)
    lag = run(both(15, (1, 2, 3)), lag)

    def late(n):
        return (16 * lax.rem(n, 2) + 16 - LATE + n // 2, 0)

    lag = run([late(0), late(1)], lag)
    part_copies = [
        remote(
            total.at[:, pl.ds(q * width, width)], parts.at[q - 1], part_send.at[q - 1], part_recv.at[q - 1],
            at(0, 0, 0, SIDE - q),
        )
        for q in (1, 3, 2)
    ]
    for copy in part_copies:
        copy.start()
    rounds = (2 * LATE - 4) // 6
    lag = loop(0, rounds, 1, lambda m: [late(6 * m + 2 + c) for c in range(6)], lag)
    lag = run([late(2 * LATE - 2), late(2 * LATE - 1)], lag)
    sum_stage(*lag[0], 0)
    exp_stage(1)
    sum_stage(*lag[1], 1)
    for copy in loads[3:]:
        copy.wait()
    residual, direction = residual_ref[...], direction_ref[...]
    image = total[:, 0:width] + noise_ref[...] * direction
    for copy, q in zip(part_copies, (1, 3, 2)):
        copy.wait_recv()
        image = image + parts[q - 1]

    image_ref[...] = image
    image_out = pltpu.make_async_copy(image_ref, image_hbm, in_sem.at[0])
    image_out.start()
    lane = lax.broadcasted_iota(jnp.int32, (RHS, 128), 1)
    side = lax.broadcasted_iota(jnp.int32, (RHS, 128), 0)
    packed = jnp.zeros((RHS, 128), jnp.float32)
    for n, product in enumerate((residual * residual, direction * image, residual * image, image * image)):
        packed = jnp.where(lane == RHS * n + side, jnp.sum(product, axis=1, keepdims=True), packed)
    own_sums[...] = jnp.sum(packed, axis=0, keepdims=True)
    sl_copies = [
        remote(own_sums, sums_line.at[n], sl_send.at[n], sl_recv.at[n], row_line[n]) for n in range(len(row_line))
    ]
    for copy in sl_copies:
        copy.start()
    for copy in line_near + line_far + sum(waves, []) + part_copies:
        copy.wait_send()
    for p in range(16):
        pair_copy(p).wait_send()
    for copy in sl_copies:
        copy.wait_recv()
    line_sums[...] = own_sums[...] + jnp.sum(sums_line[...], axis=0)
    sp_copies = [
        remote(line_sums, sums_plane.at[n], sp_send.at[n], sp_recv.at[n], plane[n]) for n in range(len(plane))
    ]
    for copy in sp_copies:
        copy.start()
    for copy in sl_copies:
        copy.wait_send()
    image_out.wait()
    for copy in sp_copies:
        copy.wait_recv()
    packed = line_sums[...] + jnp.sum(sums_plane[...], axis=0)

    norm_old, curvature, mixed, square = (
        jnp.sum(jnp.where(lane == RHS * n + side, packed, 0.0), axis=1, keepdims=True) for n in range(4)
    )
    step_size = norm_old / curvature
    norm_new = norm_old + step_size * (step_size * square - 2.0 * mixed)
    step_ref[...] = jnp.broadcast_to(step_size, step_ref.shape)
    growth_ref[...] = jnp.broadcast_to(norm_new / norm_old, growth_ref.shape)

    for copy in sp_copies:
        copy.wait_send()


def local(points, lengths, noise_var, solution, residual, direction):
    width = points.shape[1]
    out = jax.ShapeDtypeStruct((RHS, width), jnp.float32)
    vmem, dma = pltpu.VMEM, pltpu.SemaphoreType.DMA
    wide = vmem((RHS, width), jnp.float32)
    image, step_size, growth = pl.pallas_call(
        kernel,
        out_shape=(out, out, out),
        in_specs=[pl.BlockSpec(memory_space=pl.ANY)] * 5,
        out_specs=(pl.BlockSpec(memory_space=pl.ANY),) + (pl.BlockSpec(memory_space=vmem),) * 2,
        scratch_shapes=[
            wide,
            vmem((FEAT, width), jnp.bfloat16),
            vmem((1, FEAT), jnp.float32),
            vmem((1, width), jnp.float32),
            wide,
            wide,
            vmem((32, ROWS, width), jnp.bfloat16),
            vmem((SIDE - 1, FEAT, width), jnp.bfloat16),
            vmem((DEEP, SIDE * width), jnp.bfloat16),
            vmem((32, width, 128), jnp.bfloat16),
            vmem((2, width, width), jnp.float32),
            vmem((2, width, width), jnp.bfloat16),
            vmem((RHS, SIDE * width), jnp.float32),
            vmem((SIDE - 1, RHS, width), jnp.float32),
            vmem((7, 1, 128), jnp.float32),
            vmem((15, 1, 128), jnp.float32),
            vmem((1, 128), jnp.float32),
            vmem((1, 128), jnp.float32),
            dma((5,)), dma((16, 2)), dma((16, 2)), dma((16,)), dma((16,)), dma((4,)), dma((4,)),
            dma((3,)), dma((3,)), dma((7,)), dma((7,)), dma((15,)), dma((15,)),
        ],
        compiler_params=pltpu.CompilerParams(
            collective_id=0, has_side_effects=True, vmem_limit_bytes=63 << 20
        ),
        name="cg_step",
    )(points, lengths.reshape(1, FEAT), noise_var.reshape(1, width), residual, direction)
    new_residual = residual - step_size * image
    return solution + step_size * direction, new_residual, new_residual + growth * direction


def solution(mesh):
    wide = P(None, ("row", "col"))
    return jax.shard_map(
        local,
        mesh=mesh,
        in_specs=(wide, P(), P(("row", "col")), wide, wide, wide),
        out_specs=(wide, wide, wide),
        check_vma=False,
    )
```

```python
import functools

import jax
import jax.numpy as jnp
from jax import lax
from jax.experimental import pallas as pl
from jax.experimental.pallas import tpu as pltpu
from jax.sharding import PartitionSpec as P

MESH = pl.DeviceIdType.MESH
FEAT = 64
RHS = 16
DEEP = FEAT + 16
ROWS = DEEP + RHS
SIDE = 4
LATE = 13

ORDER = (
    (0, 0), (1, 0), (3, 0), (0, 1), (0, 3), (2, 0), (1, 1), (1, 3),
    (3, 1), (3, 3), (0, 2), (1, 2), (3, 2), (2, 1), (2, 3), (2, 2),
)
SLOT = {offset: n for n, offset in enumerate(ORDER)}
WAVES = (
    [((0, 0), step, step, None) for step in ((1, 0), (3, 0), (0, 1), (0, 3))],
    [
        ((1, 0), (0, 1), (1, 1), None), ((3, 0), (0, 1), (3, 1), None),
        ((1, 0), (0, 3), (1, 3), None), ((3, 0), (0, 3), (3, 3), None),
        ((1, 0), (1, 0), (2, 0), 0), ((3, 0), (3, 0), (2, 0), 1),
        ((0, 1), (0, 1), (0, 2), 0), ((0, 3), (0, 3), (0, 2), 1),
    ],
    [
        ((2, 0), (0, 1), (2, 1), None), ((2, 0), (0, 3), (2, 3), None),
        ((1, 1), (0, 1), (1, 2), 0), ((1, 3), (0, 3), (1, 2), 1),
        ((3, 1), (0, 1), (3, 2), 0), ((3, 3), (0, 3), (3, 2), 1),
    ],
    [((2, 1), (0, 1), (2, 2), 0), ((2, 3), (0, 3), (2, 2), 1)],
)


def bias_rows(scaled, flip):
    values = scaled.astype(jnp.float32)
    half = -0.5 * jnp.sum(values * values, axis=0, keepdims=True)
    high = half.astype(jnp.bfloat16).astype(jnp.float32)
    rest = half - high
    middle = rest.astype(jnp.bfloat16).astype(jnp.float32)
    low = rest - middle
    width = scaled.shape[1]
    index = lax.broadcasted_iota(jnp.int32, (16, width), 0)
    first = 3 if flip else 0
    ones = 0 if flip else 3
    rows = jnp.where(index == first, high, 0.0)
    rows = jnp.where(index == first + 1, middle, rows)
    rows = jnp.where(index == first + 2, low, rows)
    rows = jnp.where((index >= ones) & (index < ones + 3), 1.0, rows)
    return rows.astype(jnp.bfloat16)


def kernel(
    points_hbm, lengths_hbm, noise_hbm, residual_hbm, direction_hbm,
    image_hbm, step_ref, growth_ref,
    image_ref, points_ref, lengths_ref, noise_ref, residual_ref, direction_ref,
    blocks, line, weights, lefts, cross, tiles, total, parts, sums_line, sums_plane, own_sums, line_sums,
    in_sem, plane_send, plane_recv, pair_send, pair_recv, line_send, line_recv,
    part_send, part_recv, sl_send, sl_recv, sp_send, sp_recv,
):
    width = points_ref.shape[1]
    row, col = lax.axis_index("row"), lax.axis_index("col")
    core = lax.rem(row, 2)
    chip = row // 2
    y, z = chip // SIDE, lax.rem(chip, SIDE)

    def at(first, second, dcore, dx):
        dy = first * core + second * (1 - core)
        dz = first * (1 - core) + second * core
        ny, nz = lax.rem(y + dy, SIDE), lax.rem(z + dz, SIDE)
        return ((ny * SIDE + nz) * 2 + lax.rem(core + dcore, 2), lax.rem(col + dx, SIDE))

    plane = [at(a, b, 0, 0) for a, b in ORDER[1:]]
    others = [(q, c) for c in range(2) for q in range(SIDE)][1:]
    row_line = [at(0, 0, c, q) for q, c in others]
    sibling = at(0, 0, 1, 0)

    barrier = pltpu.get_barrier_semaphore()
    greeted = plane[:4] + [at(0, 0, 0, 1), at(0, 0, 0, 3), sibling]
    for device in greeted:
        pl.semaphore_signal(barrier, inc=1, device_id=device, device_id_type=MESH)

    pairs = (
        (points_hbm, points_ref), (lengths_hbm, lengths_ref), (direction_hbm, direction_ref),
        (noise_hbm, noise_ref), (residual_hbm, residual_ref),
    )
    loads = [pltpu.make_async_copy(src, dst, in_sem.at[n]) for n, (src, dst) in enumerate(pairs)]
    for copy in loads:
        copy.start()
    total[...] = jnp.zeros_like(total)
    cross[1] = jnp.full(cross.shape[1:], -1e4, jnp.float32)
    tiles[0] = jnp.zeros(tiles.shape[1:], jnp.bfloat16)
    for copy in loads[:3]:
        copy.wait()

    diagonal = lax.broadcasted_iota(jnp.int32, (FEAT, FEAT), 0) == lax.broadcasted_iota(
        jnp.int32, (FEAT, FEAT), 1
    )
    lengths = jnp.sum(jnp.where(diagonal, lengths_ref[...], 0.0), axis=1, keepdims=True)
    scaled = (points_ref[...].astype(jnp.float32) / lengths).astype(jnp.bfloat16)
    blocks[0, 0:FEAT, :] = scaled
    blocks[0, FEAT:DEEP, :] = bias_rows(scaled, False)
    blocks[0, DEEP:ROWS, :] = direction_ref[...].astype(jnp.bfloat16)

    pl.semaphore_wait(barrier, len(greeted))

    def remote(src, dst, send, recv, device):
        return pltpu.make_async_remote_copy(
            src_ref=src, dst_ref=dst, send_sem=send, recv_sem=recv, device_id=device, device_id_type=MESH
        )

    def plane_copy(src, step, dst, half):
        rows = pl.ds(0, ROWS) if half is None else pl.ds(half * (ROWS // 2), ROWS // 2)
        return remote(
            blocks.at[SLOT[src], rows], blocks.at[SLOT[dst], rows], plane_send.at[SLOT[dst], half or 0],
            plane_recv.at[SLOT[dst], half or 0], at(*step, 0, 0),
        )

    waves = [[plane_copy(*entry) for entry in wave] for wave in WAVES]

    def pair_copy(p):
        return remote(blocks.at[p], blocks.at[16 + p], pair_send.at[p], pair_recv.at[p], sibling)

    def next_wave(n):
        for copy in waves[n]:
            copy.wait_recv()
        for slot in sorted({SLOT[entry[2]] for entry in WAVES[n]}):
            pair_copy(slot).start()
        if n + 1 < len(waves):
            for copy in waves[n + 1]:
                copy.start()

    line_near = [
        remote(blocks.at[0, pl.ds(0, FEAT)], line.at[q - 1], line_send.at[n], line_recv.at[n], at(0, 0, 0, q))
        for n, q in enumerate((1, 3))
    ]
    line_far = [
        remote(
            line.at[q - 1, pl.ds(n * (FEAT // 2), FEAT // 2)], line.at[1, pl.ds(n * (FEAT // 2), FEAT // 2)],
            line_send.at[2 + n], line_recv.at[2 + n], at(0, 0, 0, q),
        )
        for n, q in enumerate((1, 3))
    ]
    pair_copy(0).start()
    for copy in line_near + waves[0]:
        copy.start()

    def transpose(block):
        lefts[block, :, 0:DEEP] = blocks[block, 0:DEEP, :].T

    def set_rows(q, part):
        weights[0:FEAT, q * width : (q + 1) * width] = part
        weights[FEAT:DEEP, q * width : (q + 1) * width] = bias_rows(part, True)

    def cross_stage(block, q, slot):
        cross[slot] = jnp.dot(
            lefts[block, :, 0:DEEP], weights[:, q * width : (q + 1) * width], preferred_element_type=jnp.float32
        )

    def exp_stage(slot):
        tiles[slot] = jnp.exp(cross[slot]).astype(jnp.bfloat16)

    def sum_stage(block, q, slot):
        columns = pl.ds(pl.multiple_of(q * width, width), width)
        total[:, columns] += jnp.dot(
            blocks[block, DEEP:ROWS, :], tiles[slot], preferred_element_type=jnp.float32
        )

    def run(chunks, before, middle=None):
        lagged = before + chunks
        for c, (block, q) in enumerate(chunks):
            sum_stage(*lagged[c], c % 2)
            exp_stage((c + 1) % 2)
            cross_stage(block, q, c % 2)
            if middle is not None and c == len(chunks) // 2 - 1:
                middle()
        return chunks[-2:]

    def loop(first, last, step, chunks_of, before, top=None, middle=None):
        def body(n, carry):
            p = first + step * n
            if top is not None:
                top(p)
            own = chunks_of(p - step)[-2:]
            lag = [
                (jnp.where(n == 0, old[0], new[0]), jnp.where(n == 0, old[1], new[1]))
                for old, new in zip(before, own)
            ]
            run(chunks_of(p), lag, None if middle is None else functools.partial(middle, p))
            return carry

        lax.fori_loop(0, (last - first) // step, body, 0)
        return chunks_of(last - step)[-2:]

    def both(p, parts_):
        return [(block, q) for block in (p, 16 + p) for q in parts_]

    set_rows(0, scaled)
    transpose(0)
    pair_copy(0).wait_recv()
    transpose(16)
    lag = run([(0, 0), (16, 0)], [(0, 0), (0, 0)])
    for near, far in zip(line_near, line_far):
        near.wait_recv()
        far.start()
    set_rows(1, line[0])
    set_rows(3, line[2])
    lag = run([(0, 1), (16, 1), (0, 3), (16, 3)], lag)
    next_wave(0)
    for p in range(1, 5):
        transpose(p)

    def pair_arrives(p):
        pair_copy(p).wait_recv()
        transpose(16 + p)

    def two_arrive(p):
        pair_arrives(p)
        pair_arrives(p + 1)

    def two(p, parts_):
        return both(p, parts_) + both(p + 1, parts_)

    def two_follow(last, p):
        transpose(jnp.minimum(p + 2, last))
        transpose(jnp.minimum(p + 3, last))

    early = [(p, q) for p in range(1, 5) for q in ((0, 1, 3) if p < 3 else (1, 3))]
    lag = run(early, lag)
    two_arrive(1)
    two_arrive(3)
    lag = run([(16 + p, q) for p, q in early], lag)
    for copy in line_far:
        copy.wait_recv()
    set_rows(2, line[1])
    far = [chunk for p in range(5) for chunk in both(p, (2,))]
    lag = run(far[:4], lag)
    next_wave(1)
    transpose(5)
    transpose(6)
    lag = run(far[4:], lag)

    def arrives(p):
        pl.when(p == 9)(functools.partial(next_wave, 2))
        pl.when(p == 13)(functools.partial(next_wave, 3))
        two_arrive(p)

    lag = loop(5, 15, 2, lambda p: two(p, (1, 2, 3)), lag, arrives, functools.partial(two_follow, 15))
    pair_arrives(15)
    lag = run(both(15, (1, 2, 3)), lag)

    def late(n):
        return (16 * lax.rem(n, 2) + 16 - LATE + n // 2, 0)

    lag = run([late(0), late(1)], lag)
    part_copies = [
        remote(
            total.at[:, pl.ds(q * width, width)], parts.at[q - 1], part_send.at[q - 1], part_recv.at[q - 1],
            at(0, 0, 0, SIDE - q),
        )
        for q in (1, 3, 2)
    ]
    for copy in part_copies:
        copy.start()
    lag = loop(0, (2 * LATE - 2) // 12, 1, lambda m: [late(12 * m + 2 + c) for c in range(12)], lag)
    sum_stage(*lag[0], 0)
    exp_stage(1)
    sum_stage(*lag[1], 1)
    for copy in loads[3:]:
        copy.wait()
    residual, direction = residual_ref[...], direction_ref[...]
    image = total[:, 0:width] + noise_ref[...] * direction
    for copy, q in zip(part_copies, (1, 3, 2)):
        copy.wait_recv()
        image = image + parts[q - 1]

    image_ref[...] = image
    image_out = pltpu.make_async_copy(image_ref, image_hbm, in_sem.at[0])
    image_out.start()
    lane = lax.broadcasted_iota(jnp.int32, (RHS, 128), 1)
    side = lax.broadcasted_iota(jnp.int32, (RHS, 128), 0)
    packed = jnp.zeros((RHS, 128), jnp.float32)
    for n, product in enumerate((residual * residual, direction * image, residual * image, image * image)):
        packed = jnp.where(lane == RHS * n + side, jnp.sum(product, axis=1, keepdims=True), packed)
    own_sums[...] = jnp.sum(packed, axis=0, keepdims=True)
    sl_copies = [
        remote(own_sums, sums_line.at[n], sl_send.at[n], sl_recv.at[n], row_line[n]) for n in range(len(row_line))
    ]
    for copy in sl_copies:
        copy.start()
    for copy in line_near + line_far + sum(waves, []) + part_copies:
        copy.wait_send()
    for p in range(16):
        pair_copy(p).wait_send()
    for copy in sl_copies:
        copy.wait_recv()
    line_sums[...] = own_sums[...] + jnp.sum(sums_line[...], axis=0)
    sp_copies = [
        remote(line_sums, sums_plane.at[n], sp_send.at[n], sp_recv.at[n], plane[n]) for n in range(len(plane))
    ]
    for copy in sp_copies:
        copy.start()
    for copy in sl_copies:
        copy.wait_send()
    image_out.wait()
    for copy in sp_copies:
        copy.wait_recv()
    packed = line_sums[...] + jnp.sum(sums_plane[...], axis=0)

    norm_old, curvature, mixed, square = (
        jnp.sum(jnp.where(lane == RHS * n + side, packed, 0.0), axis=1, keepdims=True) for n in range(4)
    )
    step_size = norm_old / curvature
    norm_new = norm_old + step_size * (step_size * square - 2.0 * mixed)
    step_ref[...] = jnp.broadcast_to(step_size, step_ref.shape)
    growth_ref[...] = jnp.broadcast_to(norm_new / norm_old, growth_ref.shape)

    for copy in sp_copies:
        copy.wait_send()


def local(points, lengths, noise_var, solution, residual, direction):
    width = points.shape[1]
    out = jax.ShapeDtypeStruct((RHS, width), jnp.float32)
    vmem, dma = pltpu.VMEM, pltpu.SemaphoreType.DMA
    wide = vmem((RHS, width), jnp.float32)
    image, step_size, growth = pl.pallas_call(
        kernel,
        out_shape=(out, out, out),
        in_specs=[pl.BlockSpec(memory_space=pl.ANY)] * 5,
        out_specs=(pl.BlockSpec(memory_space=pl.ANY),) + (pl.BlockSpec(memory_space=vmem),) * 2,
        scratch_shapes=[
            wide,
            vmem((FEAT, width), jnp.bfloat16),
            vmem((1, FEAT), jnp.float32),
            vmem((1, width), jnp.float32),
            wide,
            wide,
            vmem((32, ROWS, width), jnp.bfloat16),
            vmem((SIDE - 1, FEAT, width), jnp.bfloat16),
            vmem((DEEP, SIDE * width), jnp.bfloat16),
            vmem((32, width, 128), jnp.bfloat16),
            vmem((2, width, width), jnp.float32),
            vmem((2, width, width), jnp.bfloat16),
            vmem((RHS, SIDE * width), jnp.float32),
            vmem((SIDE - 1, RHS, width), jnp.float32),
            vmem((7, 1, 128), jnp.float32),
            vmem((15, 1, 128), jnp.float32),
            vmem((1, 128), jnp.float32),
            vmem((1, 128), jnp.float32),
            dma((5,)), dma((16, 2)), dma((16, 2)), dma((16,)), dma((16,)), dma((4,)), dma((4,)),
            dma((3,)), dma((3,)), dma((7,)), dma((7,)), dma((15,)), dma((15,)),
        ],
        compiler_params=pltpu.CompilerParams(
            collective_id=0, has_side_effects=True, vmem_limit_bytes=63 << 20
        ),
        name="cg_step",
    )(points, lengths.reshape(1, FEAT), noise_var.reshape(1, width), residual, direction)
    new_residual = residual - step_size * image
    return solution + step_size * direction, new_residual, new_residual + growth * direction


def solution(mesh):
    wide = P(None, ("row", "col"))
    return jax.shard_map(
        local,
        mesh=mesh,
        in_specs=(wide, P(), P(("row", "col")), wide, wide, wide),
        out_specs=(wide, wide, wide),
        check_vma=False,
    )
```

```python
import functools

import jax
import jax.numpy as jnp
from jax import lax
from jax.experimental import pallas as pl
from jax.experimental.pallas import tpu as pltpu
from jax.sharding import PartitionSpec as P

MESH = pl.DeviceIdType.MESH
FEAT = 64
RHS = 16
DEEP = FEAT + 16
ROWS = DEEP + RHS
SIDE = 4
LATE = 13

ORDER = (
    (0, 0), (1, 0), (3, 0), (0, 1), (0, 3), (2, 0), (1, 1), (1, 3),
    (3, 1), (3, 3), (0, 2), (1, 2), (3, 2), (2, 1), (2, 3), (2, 2),
)
SLOT = {offset: n for n, offset in enumerate(ORDER)}
WAVES = (
    [((0, 0), step, step, None) for step in ((1, 0), (3, 0), (0, 1), (0, 3))],
    [
        ((1, 0), (0, 1), (1, 1), None), ((3, 0), (0, 1), (3, 1), None),
        ((1, 0), (0, 3), (1, 3), None), ((3, 0), (0, 3), (3, 3), None),
        ((1, 0), (1, 0), (2, 0), 0), ((3, 0), (3, 0), (2, 0), 1),
        ((0, 1), (0, 1), (0, 2), 0), ((0, 3), (0, 3), (0, 2), 1),
    ],
    [
        ((2, 0), (0, 1), (2, 1), None), ((2, 0), (0, 3), (2, 3), None),
        ((1, 1), (0, 1), (1, 2), 0), ((1, 3), (0, 3), (1, 2), 1),
        ((3, 1), (0, 1), (3, 2), 0), ((3, 3), (0, 3), (3, 2), 1),
    ],
    [((2, 1), (0, 1), (2, 2), 0), ((2, 3), (0, 3), (2, 2), 1)],
)


def bias_rows(scaled, flip):
    values = scaled.astype(jnp.float32)
    half = -0.5 * jnp.sum(values * values, axis=0, keepdims=True)
    high = half.astype(jnp.bfloat16).astype(jnp.float32)
    rest = half - high
    middle = rest.astype(jnp.bfloat16).astype(jnp.float32)
    low = rest - middle
    width = scaled.shape[1]
    index = lax.broadcasted_iota(jnp.int32, (16, width), 0)
    first = 3 if flip else 0
    ones = 0 if flip else 3
    rows = jnp.where(index == first, high, 0.0)
    rows = jnp.where(index == first + 1, middle, rows)
    rows = jnp.where(index == first + 2, low, rows)
    rows = jnp.where((index >= ones) & (index < ones + 3), 1.0, rows)
    return rows.astype(jnp.bfloat16)


def kernel(
    points_hbm, lengths_hbm, noise_hbm, residual_hbm, direction_hbm,
    image_hbm, step_ref, growth_ref,
    image_ref, points_ref, lengths_ref, noise_ref, residual_ref, direction_ref,
    blocks, line, weights, lefts, cross, tiles, total, parts, sums_line, sums_plane, own_sums, line_sums,
    in_sem, plane_send, plane_recv, pair_send, pair_recv, line_send, line_recv,
    part_send, part_recv, sl_send, sl_recv, sp_send, sp_recv,
):
    width = points_ref.shape[1]
    row, col = lax.axis_index("row"), lax.axis_index("col")
    core = lax.rem(row, 2)
    chip = row // 2
    y, z = chip // SIDE, lax.rem(chip, SIDE)

    def at(first, second, dcore, dx):
        dy = first * core + second * (1 - core)
        dz = first * (1 - core) + second * core
        ny, nz = lax.rem(y + dy, SIDE), lax.rem(z + dz, SIDE)
        return ((ny * SIDE + nz) * 2 + lax.rem(core + dcore, 2), lax.rem(col + dx, SIDE))

    plane = [at(a, b, 0, 0) for a, b in ORDER[1:]]
    others = [(q, c) for c in range(2) for q in range(SIDE)][1:]
    row_line = [at(0, 0, c, q) for q, c in others]
    sibling = at(0, 0, 1, 0)

    barrier = pltpu.get_barrier_semaphore()
    greeted = plane[:4] + [at(0, 0, 0, 1), at(0, 0, 0, 3), sibling]
    for device in greeted:
        pl.semaphore_signal(barrier, inc=1, device_id=device, device_id_type=MESH)

    pairs = (
        (points_hbm, points_ref), (lengths_hbm, lengths_ref), (direction_hbm, direction_ref),
        (noise_hbm, noise_ref), (residual_hbm, residual_ref),
    )
    loads = [pltpu.make_async_copy(src, dst, in_sem.at[n]) for n, (src, dst) in enumerate(pairs)]
    for copy in loads:
        copy.start()
    total[...] = jnp.zeros_like(total)
    cross[1] = jnp.full(cross.shape[1:], -1e4, jnp.float32)
    tiles[0] = jnp.zeros(tiles.shape[1:], jnp.bfloat16)
    for copy in loads[:3]:
        copy.wait()

    diagonal = lax.broadcasted_iota(jnp.int32, (FEAT, FEAT), 0) == lax.broadcasted_iota(
        jnp.int32, (FEAT, FEAT), 1
    )
    lengths = jnp.sum(jnp.where(diagonal, lengths_ref[...], 0.0), axis=1, keepdims=True)
    scaled = (points_ref[...].astype(jnp.float32) / lengths).astype(jnp.bfloat16)
    blocks[0, 0:FEAT, :] = scaled
    blocks[0, FEAT:DEEP, :] = bias_rows(scaled, False)
    blocks[0, DEEP:ROWS, :] = direction_ref[...].astype(jnp.bfloat16)

    pl.semaphore_wait(barrier, len(greeted))

    def remote(src, dst, send, recv, device):
        return pltpu.make_async_remote_copy(
            src_ref=src, dst_ref=dst, send_sem=send, recv_sem=recv, device_id=device, device_id_type=MESH
        )

    def plane_copy(src, step, dst, half):
        rows = pl.ds(0, ROWS) if half is None else pl.ds(half * (ROWS // 2), ROWS // 2)
        return remote(
            blocks.at[SLOT[src], rows], blocks.at[SLOT[dst], rows], plane_send.at[SLOT[dst], half or 0],
            plane_recv.at[SLOT[dst], half or 0], at(*step, 0, 0),
        )

    waves = [[plane_copy(*entry) for entry in wave] for wave in WAVES]

    def pair_copy(p):
        return remote(blocks.at[p], blocks.at[16 + p], pair_send.at[p], pair_recv.at[p], sibling)

    def next_wave(n):
        for copy in waves[n]:
            copy.wait_recv()
        for slot in sorted({SLOT[entry[2]] for entry in WAVES[n]}):
            pair_copy(slot).start()
        if n + 1 < len(waves):
            for copy in waves[n + 1]:
                copy.start()

    line_near = [
        remote(blocks.at[0, pl.ds(0, FEAT)], line.at[q - 1], line_send.at[n], line_recv.at[n], at(0, 0, 0, q))
        for n, q in enumerate((1, 3))
    ]
    line_far = [
        remote(
            line.at[q - 1, pl.ds(n * (FEAT // 2), FEAT // 2)], line.at[1, pl.ds(n * (FEAT // 2), FEAT // 2)],
            line_send.at[2 + n], line_recv.at[2 + n], at(0, 0, 0, q),
        )
        for n, q in enumerate((1, 3))
    ]
    pair_copy(0).start()
    for copy in line_near + waves[0]:
        copy.start()

    def transpose(block):
        lefts[block, :, 0:DEEP] = blocks[block, 0:DEEP, :].T

    def set_rows(q, part):
        weights[0:FEAT, q * width : (q + 1) * width] = part
        weights[FEAT:DEEP, q * width : (q + 1) * width] = bias_rows(part, True)

    def cross_stage(block, q, slot):
        cross[slot] = jnp.dot(
            lefts[block, :, 0:DEEP], weights[:, q * width : (q + 1) * width], preferred_element_type=jnp.float32
        )

    def exp_stage(slot):
        tiles[slot] = jnp.exp(cross[slot]).astype(jnp.bfloat16)

    def sum_stage(block, q, slot):
        columns = pl.ds(pl.multiple_of(q * width, width), width)
        total[:, columns] += jnp.dot(
            blocks[block, DEEP:ROWS, :], tiles[slot], preferred_element_type=jnp.float32
        )

    def run(chunks, before, middle=None):
        lagged = before + chunks
        for c, (block, q) in enumerate(chunks):
            sum_stage(*lagged[c], c % 2)
            exp_stage((c + 1) % 2)
            cross_stage(block, q, c % 2)
            if middle is not None and c == len(chunks) // 2 - 1:
                middle()
        return chunks[-2:]

    def loop(first, last, step, chunks_of, before, top=None, middle=None):
        def body(n, carry):
            p = first + step * n
            if top is not None:
                top(p)
            own = chunks_of(p - step)[-2:]
            lag = [
                (jnp.where(n == 0, old[0], new[0]), jnp.where(n == 0, old[1], new[1]))
                for old, new in zip(before, own)
            ]
            run(chunks_of(p), lag, None if middle is None else functools.partial(middle, p))
            return carry

        lax.fori_loop(0, (last - first) // step, body, 0)
        return chunks_of(last - step)[-2:]

    def both(p, parts_):
        return [(block, q) for block in (p, 16 + p) for q in parts_]

    set_rows(0, scaled)
    transpose(0)
    pair_copy(0).wait_recv()
    transpose(16)
    lag = run([(0, 0), (16, 0)], [(0, 0), (0, 0)])
    for near, far in zip(line_near, line_far):
        near.wait_recv()
        far.start()
    set_rows(1, line[0])
    set_rows(3, line[2])
    lag = run([(0, 1), (16, 1), (0, 3), (16, 3)], lag)
    next_wave(0)
    for p in range(1, 5):
        transpose(p)

    def pair_arrives(p):
        pair_copy(p).wait_recv()
        transpose(16 + p)

    def two_arrive(p):
        pair_arrives(p)
        pair_arrives(p + 1)

    def two(p, parts_):
        return both(p, parts_) + both(p + 1, parts_)

    def two_follow(last, p):
        transpose(jnp.minimum(p + 2, last))
        transpose(jnp.minimum(p + 3, last))

    early = [(p, q) for p in range(1, 5) for q in ((0, 1, 3) if p < 3 else (1, 3))]
    lag = run(early, lag)
    two_arrive(1)
    two_arrive(3)
    lag = run([(16 + p, q) for p, q in early], lag)
    for copy in line_far:
        copy.wait_recv()
    set_rows(2, line[1])
    far = [chunk for p in range(5) for chunk in both(p, (2,))]
    lag = run(far, lag)
    next_wave(1)
    transpose(5)
    transpose(6)
    second = [(p, q) for p in (5, 6) for q in (1, 2, 3)]
    lag = run(second, lag)
    two_arrive(5)
    lag = run([(16 + p, q) for p, q in second], lag, functools.partial(two_follow, 15, 5))

    def arrives(p):
        pl.when(p == 9)(functools.partial(next_wave, 2))
        pl.when(p == 13)(functools.partial(next_wave, 3))
        two_arrive(p)

    lag = loop(7, 15, 2, lambda p: two(p, (1, 2, 3)), lag, arrives, functools.partial(two_follow, 15))
    pair_arrives(15)
    lag = run(both(15, (1, 2, 3)), lag)

    def late(n):
        return (16 * lax.rem(n, 2) + 16 - LATE + n // 2, 0)

    lag = run([late(0), late(1)], lag)
    part_copies = [
        remote(
            total.at[:, pl.ds(q * width, width)], parts.at[q - 1], part_send.at[q - 1], part_recv.at[q - 1],
            at(0, 0, 0, SIDE - q),
        )
        for q in (1, 3, 2)
    ]
    for copy in part_copies:
        copy.start()
    lag = loop(0, (2 * LATE - 2) // 12, 1, lambda m: [late(12 * m + 2 + c) for c in range(12)], lag)
    sum_stage(*lag[0], 0)
    exp_stage(1)
    sum_stage(*lag[1], 1)
    for copy in loads[3:]:
        copy.wait()
    residual, direction = residual_ref[...], direction_ref[...]
    image = total[:, 0:width] + noise_ref[...] * direction
    for copy, q in zip(part_copies, (1, 3, 2)):
        copy.wait_recv()
        image = image + parts[q - 1]

    image_ref[...] = image
    image_out = pltpu.make_async_copy(image_ref, image_hbm, in_sem.at[0])
    image_out.start()
    lane = lax.broadcasted_iota(jnp.int32, (RHS, 128), 1)
    side = lax.broadcasted_iota(jnp.int32, (RHS, 128), 0)
    packed = jnp.zeros((RHS, 128), jnp.float32)
    for n, product in enumerate((residual * residual, direction * image, residual * image, image * image)):
        packed = jnp.where(lane == RHS * n + side, jnp.sum(product, axis=1, keepdims=True), packed)
    own_sums[...] = jnp.sum(packed, axis=0, keepdims=True)
    sl_copies = [
        remote(own_sums, sums_line.at[n], sl_send.at[n], sl_recv.at[n], row_line[n]) for n in range(len(row_line))
    ]
    for copy in sl_copies:
        copy.start()
    for copy in line_near + line_far + sum(waves, []) + part_copies:
        copy.wait_send()
    for p in range(16):
        pair_copy(p).wait_send()
    for copy in sl_copies:
        copy.wait_recv()
    line_sums[...] = own_sums[...] + jnp.sum(sums_line[...], axis=0)
    sp_copies = [
        remote(line_sums, sums_plane.at[n], sp_send.at[n], sp_recv.at[n], plane[n]) for n in range(len(plane))
    ]
    for copy in sp_copies:
        copy.start()
    for copy in sl_copies:
        copy.wait_send()
    image_out.wait()
    for copy in sp_copies:
        copy.wait_recv()
    packed = line_sums[...] + jnp.sum(sums_plane[...], axis=0)

    norm_old, curvature, mixed, square = (
        jnp.sum(jnp.where(lane == RHS * n + side, packed, 0.0), axis=1, keepdims=True) for n in range(4)
    )
    step_size = norm_old / curvature
    norm_new = norm_old + step_size * (step_size * square - 2.0 * mixed)
    step_ref[...] = jnp.broadcast_to(step_size, step_ref.shape)
    growth_ref[...] = jnp.broadcast_to(norm_new / norm_old, growth_ref.shape)

    for copy in sp_copies:
        copy.wait_send()


def local(points, lengths, noise_var, solution, residual, direction):
    width = points.shape[1]
    out = jax.ShapeDtypeStruct((RHS, width), jnp.float32)
    vmem, dma = pltpu.VMEM, pltpu.SemaphoreType.DMA
    wide = vmem((RHS, width), jnp.float32)
    image, step_size, growth = pl.pallas_call(
        kernel,
        out_shape=(out, out, out),
        in_specs=[pl.BlockSpec(memory_space=pl.ANY)] * 5,
        out_specs=(pl.BlockSpec(memory_space=pl.ANY),) + (pl.BlockSpec(memory_space=vmem),) * 2,
        scratch_shapes=[
            wide,
            vmem((FEAT, width), jnp.bfloat16),
            vmem((1, FEAT), jnp.float32),
            vmem((1, width), jnp.float32),
            wide,
            wide,
            vmem((32, ROWS, width), jnp.bfloat16),
            vmem((SIDE - 1, FEAT, width), jnp.bfloat16),
            vmem((DEEP, SIDE * width), jnp.bfloat16),
            vmem((32, width, 128), jnp.bfloat16),
            vmem((2, width, width), jnp.float32),
            vmem((2, width, width), jnp.bfloat16),
            vmem((RHS, SIDE * width), jnp.float32),
            vmem((SIDE - 1, RHS, width), jnp.float32),
            vmem((7, 1, 128), jnp.float32),
            vmem((15, 1, 128), jnp.float32),
            vmem((1, 128), jnp.float32),
            vmem((1, 128), jnp.float32),
            dma((5,)), dma((16, 2)), dma((16, 2)), dma((16,)), dma((16,)), dma((4,)), dma((4,)),
            dma((3,)), dma((3,)), dma((7,)), dma((7,)), dma((15,)), dma((15,)),
        ],
        compiler_params=pltpu.CompilerParams(
            collective_id=0, has_side_effects=True, vmem_limit_bytes=63 << 20
        ),
        name="cg_step",
    )(points, lengths.reshape(1, FEAT), noise_var.reshape(1, width), residual, direction)
    new_residual = residual - step_size * image
    return solution + step_size * direction, new_residual, new_residual + growth * direction


def solution(mesh):
    wide = P(None, ("row", "col"))
    return jax.shard_map(
        local,
        mesh=mesh,
        in_specs=(wide, P(), P(("row", "col")), wide, wide, wide),
        out_specs=(wide, wide, wide),
        check_vma=False,
    )
```
